32 devices in a mesh: dp: 16 (over z, x, core), tensor: 2 (over y).
Axes of the slice: x: 2, y: 2, z: 4, core: 2. Of those that a mesh axis runs over, the one named last changes fastest.
Arguments:
- clips: bfloat16 [16, 8, 8, 16, 1024], P('dp', None, None, None, 'tensor'), may hold values from -6 to 6
- out_grad: bfloat16 [16, 8, 8, 16, 1024], P('dp', None, None, None, 'tensor'), may hold values from -6 to 6
- spatial_weight: bfloat16 [3, 3, 1024, 1024], P(None, None, None, 'tensor'), may hold values from -0.0625 to 0.0625
- temporal_weight: bfloat16 [3, 1024, 1024], P(None, 'tensor'), may hold values from -0.109375 to 0.109375
Outputs:
- mixed: bfloat16 [16, 8, 8, 16, 1024], P('dp', None, None, None, 'tensor')
- clip_grad: bfloat16 [16, 8, 8, 16, 1024], P('dp', None, None, None, 'tensor')
- spatial_grad: bfloat16 [3, 3, 1024, 1024], P(None, None, 'dp', 'tensor')
- temporal_grad: bfloat16 [3, 1024, 1024], P(None, 'tensor', 'dp')
The draws below stay inside these ranges and needn't reach their ends.
All inputs are finite; a program needn't handle non-finite values.
Results may differ from the reference program's by a relative error of at most 0.006.
Values may be sent and summed in bfloat16 or wider, within the bound.
A program may use at most 128 MiB of HBM per device.

```python
import jax
import jax.numpy as jnp
from jax import lax

C = 1024
GS = 32
FRAMES = 8
HEIGHT = 8
BREADTH = 16
CLIPS = 16
POSITIONS = 16384


def with_spikes(entries, key, source, target, parts, factor):
    owner, partner = [(jnp.arange(entries.shape[dim]) // (entries.shape[dim] // parts)).reshape([-1 if axis == dim else 1 for axis in range(entries.ndim)]) for dim in (source, target)]
    chosen = jax.random.permutation(key, parts)[partner]
    strong = (owner == chosen) | (owner == (partner + parts // 2) % parts)
    return jnp.where(strong, factor * entries, entries)


def levels(rng, shape, cuts, least, top_value):
    def one(axis_at, blocks):
        steps = jax.random.uniform(jax.random.fold_in(jax.random.fold_in(rng, 6), axis_at), (blocks,), jnp.float32, least / len(cuts), top_value / len(cuts))
        return jnp.repeat(jnp.exp(steps), shape[axis_at] // blocks).reshape((-1,) + (1,) * (len(shape) - axis_at - 1))

    gain = one(*cuts[0])
    for cut in cuts[1:]:
        gain = gain * one(*cut)
    return gain


def noise(key, extent, deviation, most, split=(), held_as=jnp.bfloat16):
    values = deviation * jax.random.normal(key, extent, jnp.float32)
    if split:
        values = values * levels(key, extent, split, -0.22, 0.18)
    return jnp.clip(values, -most, most).astype(held_as)


def noise_with(rng, shape, deviation, reach, cuts, heavy, held_as=jnp.bfloat16):
    entries = deviation * jax.random.normal(rng, shape, jnp.float32)
    if cuts:
        entries = entries * levels(rng, shape, cuts, -0.22, 0.18)
    return jnp.clip(with_spikes(entries, jax.random.fold_in(rng, 3), *heavy), -reach, reach).astype(held_as)


def setup_inputs(seed: int = 0) -> dict:
    keys = jax.random.split(jax.random.key(seed), 5)
    clips = noise_with(keys[0], (CLIPS, FRAMES, HEIGHT, BREADTH, C), 1.0, 6.0, ((0, 16), (4, 2)), (0, 4, 16, 2.0))
    out_grad = noise_with(keys[1], (CLIPS, FRAMES, HEIGHT, BREADTH, C), 1.0, 6.0, ((0, 16), (4, 2)), (0, 4, 16, 2.0))
    spatial_weight = noise(keys[2], (3, 3, C, C), (9 * C) ** -0.5, 0.0625, ((3, 2),))
    temporal_weight = noise(keys[3], (3, C, C), (3 * C) ** -0.5, 0.109375, ((1, 2),))
    return {"clips": clips, "out_grad": out_grad, "spatial_weight": spatial_weight, "temporal_weight": temporal_weight}


def group_silu(values):
    shaped = values.reshape(values.shape[0], -1, values.shape[-1] // GS, GS)
    center = lax.optimization_barrier(jnp.mean(shaped, axis=(1, 3), keepdims=True))
    offsets = shaped - center
    spread = lax.optimization_barrier(jnp.mean(offsets * offsets, axis=(1, 3), keepdims=True))
    return jax.nn.silu(offsets * lax.rsqrt(spread + 1e-05)).reshape(values.shape)

def spatial_conv(inputs, kernel):
    dims = inputs.shape
    flat = inputs.reshape((dims[0] * dims[1], dims[2], dims[3], dims[4]))
    result = lax.conv_general_dilated(flat, kernel, (1, 1), ((1, 1), (1, 1)), dimension_numbers=('NHWC', 'HWIO', 'NHWC'), preferred_element_type=jnp.float32)
    return result.reshape(dims[:4] + (kernel.shape[3],))

def flipped(kernel):
    return jnp.transpose(kernel[::-1, ::-1], (0, 1, 3, 2))

def spatial_wgrad(inputs, grads):
    dims = inputs.shape
    padded = jnp.pad(inputs, ((0, 0), (0, 0), (1, 1), (1, 1), (0, 0)))
    right_side = grads.reshape(-1, grads.shape[-1])
    collected = []
    for row_tap in range(3):
        for col_tap in range(3):
            window = padded[:, :, row_tap:row_tap + dims[2], col_tap:col_tap + dims[3]].reshape(-1, dims[4])
            collected.append(lax.dot_general(window, right_side, (((0,), (0,)), ((), ())), preferred_element_type=jnp.float32))
    return jnp.stack(collected).reshape(3, 3, dims[4], grads.shape[-1])

def temporal_conv(inputs, kernel):
    frame_count = inputs.shape[1]
    padded = jnp.pad(inputs, ((0, 0), (1, 1), (0, 0), (0, 0), (0, 0)))
    result = jnp.zeros((inputs.size // inputs.shape[-1], kernel.shape[2]), jnp.float32)
    for kernel_tap in range(3):
        window = padded[:, kernel_tap:kernel_tap + frame_count].reshape(-1, inputs.shape[-1])
        result = result + jnp.dot(window, kernel[kernel_tap], preferred_element_type=jnp.float32)
    return result.reshape(inputs.shape[:4] + (kernel.shape[2],))

def temporal_back(grads, kernel):
    frame_count = grads.shape[1]
    padded = jnp.pad(grads, ((0, 0), (1, 1), (0, 0), (0, 0), (0, 0)))
    result = jnp.zeros((grads.size // grads.shape[-1], kernel.shape[1]), jnp.float32)
    for kernel_tap in range(3):
        window = padded[:, 2 - kernel_tap:2 - kernel_tap + frame_count].reshape(-1, grads.shape[-1])
        result = result + lax.dot_general(window, kernel[kernel_tap], (((1,), (1,)), ((), ())), preferred_element_type=jnp.float32)
    return result.reshape(grads.shape[:4] + (kernel.shape[1],))

def temporal_wgrad(inputs, grads):
    frame_count = inputs.shape[1]
    padded = jnp.pad(inputs, ((0, 0), (1, 1), (0, 0), (0, 0), (0, 0)))
    right_side = grads.reshape(-1, grads.shape[-1])
    collected = []
    for kernel_tap in range(3):
        window = padded[:, kernel_tap:kernel_tap + frame_count].reshape(-1, inputs.shape[-1])
        collected.append(lax.dot_general(window, right_side, (((0,), (0,)), ((), ())), preferred_element_type=jnp.float32))
    return jnp.stack(collected)

def reference(clips, out_grad, spatial_weight, temporal_weight):
    grad_scale = 1.0 / jnp.sqrt(jnp.float32(POSITIONS))
    first_act, pull_first = jax.vjp(group_silu, clips.astype(jnp.float32))
    hidden_first = first_act.astype(jnp.bfloat16)
    spatial_out = spatial_conv(hidden_first, spatial_weight)
    second_act, pull_second = jax.vjp(group_silu, spatial_out)
    hidden_second = second_act.astype(jnp.bfloat16)
    mixed = (clips.astype(jnp.float32) + temporal_conv(hidden_second, temporal_weight)).astype(jnp.bfloat16)
    grad_second = temporal_back(out_grad, temporal_weight)
    grad_spatial = pull_second(grad_second)[0].astype(jnp.bfloat16)
    temporal_grad = (temporal_wgrad(hidden_second, out_grad) * grad_scale).astype(jnp.bfloat16)
    grad_first = spatial_conv(grad_spatial, flipped(spatial_weight))
    spatial_grad = (spatial_wgrad(hidden_first, grad_spatial) * grad_scale).astype(jnp.bfloat16)
    clip_grad = (out_grad.astype(jnp.float32) + pull_first(grad_first)[0]).astype(jnp.bfloat16)
    return (mixed, clip_grad, spatial_grad, temporal_grad)
```

```python
import jax
import jax.numpy as jnp
from jax import lax
from jax.sharding import PartitionSpec as P

GS = 32


def group_silu(values):
    shaped = values.reshape(values.shape[0], -1, values.shape[-1] // GS, GS)
    center = jnp.mean(shaped, axis=(1, 3), keepdims=True)
    offsets = shaped - center
    spread = jnp.mean(offsets * offsets, axis=(1, 3), keepdims=True)
    return jax.nn.silu(offsets * lax.rsqrt(spread + 1e-05)).reshape(values.shape)


def spatial_conv(inputs, kernel):
    dims = inputs.shape
    flat = inputs.reshape((dims[0] * dims[1], dims[2], dims[3], dims[4]))
    result = lax.conv_general_dilated(
        flat,
        kernel,
        (1, 1),
        ((1, 1), (1, 1)),
        dimension_numbers=("NHWC", "HWIO", "NHWC"),
        preferred_element_type=jnp.float32,
    )
    return result.reshape(dims[:4] + (kernel.shape[3],))


def flipped(kernel):
    return jnp.transpose(kernel[::-1, ::-1], (0, 1, 3, 2))


def spatial_wgrad(inputs, grads):
    dims = inputs.shape
    padded = jnp.pad(inputs, ((0, 0), (0, 0), (1, 1), (1, 1), (0, 0)))
    right_side = grads.reshape(-1, grads.shape[-1])
    collected = []
    for row_tap in range(3):
        for col_tap in range(3):
            window = padded[:, :, row_tap : row_tap + dims[2], col_tap : col_tap + dims[3]].reshape(
                -1, dims[4]
            )
            collected.append(
                lax.dot_general(
                    window, right_side, (((0,), (0,)), ((), ())), preferred_element_type=jnp.float32
                )
            )
    return jnp.stack(collected).reshape(3, 3, dims[4], grads.shape[-1])


def temporal_conv(inputs, kernel):
    frame_count = inputs.shape[1]
    padded = jnp.pad(inputs, ((0, 0), (1, 1), (0, 0), (0, 0), (0, 0)))
    result = jnp.zeros((inputs.size // inputs.shape[-1], kernel.shape[2]), jnp.float32)
    for kernel_tap in range(3):
        window = padded[:, kernel_tap : kernel_tap + frame_count].reshape(-1, inputs.shape[-1])
        result = result + jnp.dot(window, kernel[kernel_tap], preferred_element_type=jnp.float32)
    return result.reshape(inputs.shape[:4] + (kernel.shape[2],))


def temporal_back(grads, kernel):
    frame_count = grads.shape[1]
    padded = jnp.pad(grads, ((0, 0), (1, 1), (0, 0), (0, 0), (0, 0)))
    result = jnp.zeros((grads.size // grads.shape[-1], kernel.shape[1]), jnp.float32)
    for kernel_tap in range(3):
        window = padded[:, 2 - kernel_tap : 2 - kernel_tap + frame_count].reshape(
            -1, grads.shape[-1]
        )
        result = result + lax.dot_general(
            window, kernel[kernel_tap], (((1,), (1,)), ((), ())), preferred_element_type=jnp.float32
        )
    return result.reshape(grads.shape[:4] + (kernel.shape[1],))


def temporal_wgrad(inputs, grads):
    frame_count = inputs.shape[1]
    padded = jnp.pad(inputs, ((0, 0), (1, 1), (0, 0), (0, 0), (0, 0)))
    right_side = grads.reshape(-1, grads.shape[-1])
    collected = []
    for kernel_tap in range(3):
        window = padded[:, kernel_tap : kernel_tap + frame_count].reshape(-1, inputs.shape[-1])
        collected.append(
            lax.dot_general(
                right_side, window, (((0,), (0,)), ((), ())), preferred_element_type=jnp.float32
            )
        )
    return jnp.stack(collected)


def bit_of(index, stage):
    return (index // (1 << stage)) % 2


def swap(values, axis, stage):
    size = lax.axis_size(axis)
    return lax.ppermute(values, axis, [(d, d ^ (1 << stage)) for d in range(size)])


def gather_channels(values):
    size = lax.axis_size("tensor")
    index = lax.axis_index("tensor")
    held = values
    for stage in range(size.bit_length() - 1):
        other = swap(held, "tensor", stage)
        low = bit_of(index, stage) == 0
        held = jnp.concatenate(
            [jnp.where(low, held, other), jnp.where(low, other, held)], axis=-1
        )
    return held


def scatter_channels(values):
    size = lax.axis_size("tensor")
    index = lax.axis_index("tensor")
    held = values
    for stage in reversed(range(size.bit_length() - 1)):
        half = held.shape[-1] // 2
        low = bit_of(index, stage) == 0
        first, second = held[..., :half], held[..., half:]
        sent = jnp.where(low, second, first).astype(jnp.bfloat16)
        held = jnp.where(low, first, second) + swap(sent, "tensor", stage).astype(jnp.float32)
    return held


def scatter_rows(values):
    size = lax.axis_size("dp")
    index = lax.axis_index("dp")
    taps, rows, cols = values.shape
    held = values.reshape(taps, size, rows // size, cols)
    for stage in range(size.bit_length() - 1):
        pairs = held.reshape(taps, -1, 2, rows // size, cols)
        mine = bit_of(index, stage)
        kept = lax.dynamic_index_in_dim(pairs, mine, 2, keepdims=False)
        sent = lax.dynamic_index_in_dim(pairs, 1 - mine, 2, keepdims=False)
        got = swap(sent.astype(jnp.bfloat16), "dp", stage)
        held = kept.astype(jnp.float32) + got.astype(jnp.float32)
        if (2 << stage) < size:
            held = held.astype(jnp.bfloat16)
    return held.reshape(taps, rows // size, cols)


def per_device(clips, out_grad, spatial_weight, temporal_weight):
    position_count = (
        clips.shape[0] * clips.shape[1] * clips.shape[2] * clips.shape[3] * lax.axis_size("dp")
    )
    grad_scale = 1.0 / jnp.sqrt(jnp.float32(position_count))
    first_act, pull_first = jax.vjp(group_silu, clips.astype(jnp.float32))
    hidden_first = first_act.astype(jnp.bfloat16)
    first_full = gather_channels(hidden_first)
    spatial_out = spatial_conv(first_full, spatial_weight)
    second_act, pull_second = jax.vjp(group_silu, spatial_out)
    hidden_second = second_act.astype(jnp.bfloat16)
    temporal_out = scatter_channels(temporal_conv(hidden_second, temporal_weight))
    mixed = (clips.astype(jnp.float32) + temporal_out).astype(jnp.bfloat16)
    grad_full = gather_channels(out_grad)
    grad_second = temporal_back(grad_full, temporal_weight)
    grad_spatial = pull_second(grad_second)[0].astype(jnp.bfloat16)
    temporal_local = temporal_wgrad(hidden_second, grad_full)
    grad_partial = spatial_conv(grad_spatial, flipped(spatial_weight))
    grad_first = scatter_channels(grad_partial)
    spatial_local = spatial_wgrad(first_full, grad_spatial)
    temporal_share = jnp.transpose(scatter_rows(temporal_local.astype(jnp.bfloat16)), (0, 2, 1))
    spatial_share = jnp.stack([scatter_rows(spatial_local[tap].astype(jnp.bfloat16)) for tap in range(3)])
    clip_grad = (out_grad.astype(jnp.float32) + pull_first(grad_first)[0]).astype(jnp.bfloat16)
    spatial_out_grad = (spatial_share * grad_scale).astype(jnp.bfloat16)
    temporal_out_grad = (temporal_share * grad_scale).astype(jnp.bfloat16)
    return (mixed, clip_grad, spatial_out_grad, temporal_out_grad)


def solution(mesh):
    placed = (
        P("dp", None, None, None, "tensor"),
        P("dp", None, None, None, "tensor"),
        P(None, None, None, "tensor"),
        P(None, "tensor", None),
    )
    return jax.shard_map(
        per_device,
        mesh=mesh,
        in_specs=placed,
        out_specs=(
            P("dp", None, None, None, "tensor"),
            P("dp", None, None, None, "tensor"),
            P(None, None, "dp", "tensor"),
            P(None, "tensor", "dp"),
        ),
        check_vma=False,
    )
```

```python
import functools

import jax
import jax.numpy as jnp
from jax import lax
from jax.experimental import pallas as pl
from jax.experimental.pallas import tpu as pltpu
from jax.sharding import PartitionSpec as P

GS = 32
SLOTS = 3
MESH = pl.DeviceIdType.MESH
F32, BF16 = jnp.float32, jnp.bfloat16
NN = (((1,), (0,)), ((), ()))
NT = (((1,), (1,)), ((), ()))
TN = (((0,), (0,)), ((), ()))


def dot(left, right, dims):
    return lax.dot_general(left, right, dims, preferred_element_type=F32)


def bits_reversed(value, size):
    result, step = 0, 1
    while step < size:
        result = result * 2 + (value // step) % 2
        step *= 2
    return result


def kernel(
    T, ND, frames, height, breadth, scale,
    clips, og_in, sw_in, tw_in,
    mixed, cgrad, wgrad,
    sw, tw, first, shifted, gradsp, second, og, acc, gsec, own, ysend, tgot, fgot, same, gbuf, *rest,
):
    stages = ND.bit_length() - 1
    got = rest[:stages]
    load_sem, hf_sem, og_sem, to_sem, gf_sem, rs_send, rs_recv = rest[stages:]
    HW = height * breadth
    POS = frames * HW
    CL = clips.shape[1]
    block = wgrad.shape[1]
    per_slot = CL // block
    me_t = lax.axis_index("tensor")
    me_d = lax.axis_index("dp")
    peers = [lax.rem(me_t + j, T) for j in range(T)]
    owners = [lax.rem(me_t - j + T, T) for j in range(T)]
    bit = [lax.rem(me_d // (1 << s), 2) for s in range(stages)]
    partner = [me_d + (1 - 2 * bit[s]) * (1 << s) for s in range(stages)]

    loads = []
    for j in range(T):
        rows = pl.ds(pl.multiple_of(owners[j] * CL, CL), CL)
        loads.append(pltpu.make_async_copy(sw_in.at[:, rows, :], sw.at[:, j], load_sem.at[0, j]))
        loads.append(pltpu.make_async_copy(tw_in.at[:, :, rows], tw.at[:, j], load_sem.at[1, j]))
    og_load = pltpu.make_async_copy(og_in, og.at[0, pl.ds(HW, POS)], load_sem.at[2, 0])
    og_load.start()
    for load in loads:
        load.start()

    barrier = pltpu.get_barrier_semaphore()
    for j in range(1, T):
        pl.semaphore_signal(barrier, inc=1, device_id={"tensor": peers[j]}, device_id_type=MESH)
    for s in range(stages):
        pl.semaphore_signal(barrier, inc=1, device_id={"dp": partner[s]}, device_id_type=MESH)

    edge = jnp.zeros((frames, breadth, CL), BF16)
    frame = jnp.zeros((HW, CL), BF16)
    for j in range(T):
        first[j, :, :breadth, :] = edge
        first[j, :, breadth + HW :, :] = edge
        og[j, :HW, :] = frame
        og[j, HW + POS :, :] = frame
    gradsp[:, :breadth, :] = edge
    gradsp[:, breadth + HW :, :] = edge
    second[:HW, :] = frame
    second[HW + POS :, :] = frame
    same[...] = jnp.where(
        lax.broadcasted_iota(jnp.int32, (CL, CL), 0) // GS
        == lax.broadcasted_iota(jnp.int32, (CL, CL), 1) // GS,
        1.0,
        0.0,
    ).astype(BF16)

    def group_mean(total):
        high = total.astype(BF16).astype(F32)
        middle = (total - high).astype(BF16).astype(F32)
        low = total - high - middle
        row = lax.broadcasted_iota(jnp.int32, (16, CL), 0)
        terms = jnp.where(row == 0, high, jnp.where(row == 1, middle, jnp.where(row == 2, low, 0.0)))
        summed = dot(terms.astype(BF16), same[...], NN)
        return jnp.sum(summed, axis=0, keepdims=True) * (1.0 / (GS * POS))

    def over_frames(body, count):
        zero = tuple(jnp.zeros((1, CL), F32) for _ in range(count))

        def step(f, sums):
            return tuple(a + jnp.sum(v, axis=0, keepdims=True) for a, v in zip(sums, body(f)))

        return lax.fori_loop(0, frames, step, zero)

    def rows_of(f, offset=0):
        return pl.ds(pl.multiple_of(f * HW + offset, HW), HW)

    def statistics(load):
        center = group_mean(over_frames(lambda f: (load(f),), 1)[0])

        def squares(f):
            offsets = load(f) - center
            return (offsets * offsets,)

        spread = group_mean(over_frames(squares, 1)[0])
        return center, lax.rsqrt(spread + 1e-05)

    def sigmoid(u):
        return 1.0 / (1.0 + jnp.exp(-u))

    def slope(u):
        s = sigmoid(u)
        return s * (1.0 + u * (1.0 - s))

    def pull_back(load, center, rate, grad, put):
        def sums(f):
            unit = (load(f) - center) * rate
            d = grad(f) * slope(unit)
            return d, d * unit

        a, b = over_frames(sums, 2)
        a, b = group_mean(a), group_mean(b)

        def write(f, carry):
            unit = (load(f) - center) * rate
            d = grad(f) * slope(unit)
            put(f, rate * (d - a - unit * b))
            return carry

        lax.fori_loop(0, frames, write, 0)

    def remote(source, target, sends, receives, device):
        return pltpu.make_async_remote_copy(
            src_ref=source, dst_ref=target, send_sem=sends, recv_sem=receives,
            device_id=device, device_id_type=MESH,
        )

    load_clip = lambda f: clips[rows_of(f), :].astype(F32)
    center1, rate1 = statistics(load_clip)
    inside = pl.ds(breadth, HW)

    def put_first(f, carry):
        unit = (load_clip(f) - center1) * rate1
        first[0, f, inside, :] = (unit * sigmoid(unit)).astype(BF16)
        return carry

    lax.fori_loop(0, frames, put_first, 0)
    pl.semaphore_wait(barrier, T - 1 + stages)
    middle = pl.ds(HW, POS)
    hf_copies, og_copies = [], []
    for j in range(1, T):
        hf_copies.append(
            remote(first.at[0, :, inside, :], first.at[j, :, inside, :],
                   hf_sem.at[0, j], hf_sem.at[1, j], {"tensor": peers[j]})
        )
        hf_copies[-1].start()
    og_load.wait()
    for j in range(1, T):
        og_copies.append(
            remote(og.at[0, middle], og.at[j, middle], og_sem.at[0, j], og_sem.at[1, j], {"tensor": peers[j]})
        )
        og_copies[-1].start()
    for load in loads:
        load.wait()

    def shift(load, target, column):
        wide = HW + 2 * breadth
        at = lax.rem(lax.broadcasted_iota(jnp.int32, (wide, CL), 0), breadth)
        keep = at != (0 if column == 0 else breadth - 1)

        def step(f, carry):
            moved = pltpu.roll(load(f).astype(F32), 1 if column == 0 else wide - 1, 0)
            shifted[target, f] = jnp.where(keep, moved, 0.0).astype(BF16)
            return carry

        lax.fori_loop(0, frames, step, 0)

    def window(ref, slot, a):
        rows = pl.ds(pl.multiple_of(a * breadth, breadth), HW)
        return (ref[:, rows, :] if slot is None else ref[slot, :, rows, :]).reshape(POS, CL)

    def conv_slot(j):
        for column in range(3):
            if column == 1:
                ref = first
            else:
                ref = shifted
                shift(lambda f: first[j, f], j, column)

            def tap(a, carry, ref=ref, column=column):
                acc[...] += dot(window(ref, j, a), sw[a * 3 + column, j], NN)
                return carry

            lax.fori_loop(0, 3, tap, 0)

    acc[...] = jnp.zeros_like(acc)
    conv_slot(0)
    for j in range(1, T):
        hf_copies[j - 1].wait_recv()
        conv_slot(j)

    load_out = lambda f: acc[rows_of(f), :]
    center2, rate2 = statistics(load_out)

    def put_second(f, carry):
        unit = (load_out(f) - center2) * rate2
        second[rows_of(f, HW), :] = (unit * sigmoid(unit)).astype(BF16)
        return carry

    lax.fori_loop(0, frames, put_second, 0)

    def temporal(j, target):
        def tap(k, carry):
            target[...] += dot(second[pl.ds(pl.multiple_of(k * HW, HW), POS), :], tw[k, j], NN)
            return carry

        target[...] = jnp.zeros_like(target)
        lax.fori_loop(0, 3, tap, 0)

    to_copies, gf_copies = [], []
    for j in range(1, T):
        temporal(j, own)
        ysend[j - 1] = own[...].astype(BF16)
        to_copies.append(
            remote(ysend.at[j - 1], tgot.at[j - 1], to_sem.at[0, j], to_sem.at[1, j], {"tensor": owners[j]})
        )
        to_copies[-1].start()
    temporal(0, own)

    def back_slot(j):
        def tap(k, carry):
            rows = pl.ds(pl.multiple_of((2 - k) * HW, HW), POS)
            gsec[...] += dot(og[j, rows, :], tw[k, j], NT)
            return carry

        lax.fori_loop(0, 3, tap, 0)

    gsec[...] = jnp.zeros_like(gsec)
    back_slot(0)

    taps = wgrad.shape[0]

    def source(s, n, half):
        size = ND >> (s + 1)
        rows = pl.ds(half * size, size)
        return gbuf.at[lax.rem(n, SLOTS), rows] if s == 0 else got[s - 1].at[n, rows]

    def exchange(s, n):
        return remote(source(s, n, 1 - bit[s]), got[s].at[n], rs_send.at[s, n], rs_recv.at[s, n],
                      {"dp": partner[s]})

    def advance(s, n):
        exchange(s - 1, n).wait_recv()
        total = got[s - 1][n].astype(F32) + source(s - 1, n, bit[s - 1])[...].astype(F32)
        if s < stages:
            got[s - 1][n] = total.astype(BF16)
            exchange(s, n).start()
        else:
            wgrad[n] = (total * scale).reshape(block, CL).astype(BF16)

    def emit(n, slots):
        @pl.when(n >= SLOTS)
        def _():
            exchange(0, n - SLOTS).wait_send()

        for j in range(T):
            place = bits_reversed(owners[j], T)
            product = slots(j)
            for b in range(per_slot):
                gbuf[lax.rem(n, SLOTS), bits_reversed(b, per_slot) * T + place] = (
                    product[b * block : (b + 1) * block].astype(BF16)
                )
        exchange(0, n).start()

        @pl.when(n >= 1)
        def _():
            advance(1, n - 1)

    for j in range(1, T):
        og_copies[j - 1].wait_recv()

    def temporal_tap(k, carry):
        rows = pl.ds(pl.multiple_of(k * HW, HW), POS)
        emit(k, lambda j: dot(og[j, middle, :], second[rows, :], TN))
        return carry

    lax.fori_loop(0, 3, temporal_tap, 0)

    for j in range(1, T):
        back_slot(j)

    def put_gradsp(f, value):
        gradsp[f, inside, :] = value.astype(BF16)

    pull_back(load_out, center2, rate2, lambda f: gsec[rows_of(f), :], put_gradsp)

    done = {s: 0 for s in range(2, stages + 1)}

    def move(s, upto):
        for n in range(done[s], min(upto, taps)):
            advance(s, n)
        done[s] = max(done[s], min(upto, taps))

    for column in range(3):
        if column == 1:
            ref = first
        else:
            ref = shifted
            for j in range(T):
                shift(lambda f, j=j: first[j, f], j, column)

        def spatial_tap(a, carry, ref=ref, column=column):
            emit(3 + column * 3 + a, lambda j: dot(window(ref, j, a), window(gradsp, None, 1), TN))
            return carry

        lax.fori_loop(0, 3, spatial_tap, 0)
        for s in range(2, stages + 1):
            move(s, 2 * column + 2 - 2 * (s - 2))
    advance(1, taps - 1)

    def grad_slot(j):
        acc[...] = jnp.zeros_like(acc)
        for column in range(3):
            if column == 1:
                ref, slot = gradsp, None
            else:
                ref, slot = shifted, 0
                shift(lambda f: gradsp[f], 0, column)

            def tap(a, carry, ref=ref, slot=slot, column=column):
                acc[...] += dot(window(ref, slot, a), sw[(2 - a) * 3 + 2 - column, j], NT)
                return carry

            lax.fori_loop(0, 3, tap, 0)

    for j in range(1, T):
        grad_slot(j)
        to_copies[j - 1].wait_send()
        ysend[j - 1] = acc[...].astype(BF16)
        gf_copies.append(
            remote(ysend.at[j - 1], fgot.at[j - 1], gf_sem.at[0, j], gf_sem.at[1, j], {"tensor": owners[j]})
        )
        gf_copies[-1].start()
    for s in range(2, stages + 1):
        move(s, 7 - (s - 2))
    grad_slot(0)
    for s in range(2, stages + 1):
        move(s, 8 - (s - 2))

    for j in range(1, T):
        to_copies[j - 1].wait_recv()

    def put_mixed(f, carry):
        rows = rows_of(f)
        total = load_clip(f) + own[rows, :]
        for j in range(1, T):
            total = total + tgot[j - 1, rows, :].astype(F32)
        mixed[rows, :] = total.astype(BF16)
        return carry

    lax.fori_loop(0, frames, put_mixed, 0)
    for s in range(2, stages + 1):
        move(s, 10 - (s - 2))

    for j in range(1, T):
        gf_copies[j - 1].wait_recv()

    def grad_first(f):
        total = acc[rows_of(f), :]
        for j in range(1, T):
            total = total + fgot[j - 1, rows_of(f), :].astype(F32)
        return total

    def put_clip(f, value):
        cgrad[rows_of(f), :] = (og[0, rows_of(f, HW), :].astype(F32) + value).astype(BF16)

    pull_back(load_clip, center1, rate1, grad_first, put_clip)

    for n in range(10, taps + stages):
        for s in range(2, stages + 1):
            move(s, n + 1 - (s - 2))

    for copy in hf_copies + og_copies + gf_copies:
        copy.wait_send()
    for n in range(max(0, taps - SLOTS), taps):
        exchange(0, n).wait_send()

    def drain(n, carry):
        for s in range(1, stages):
            exchange(s, n).wait_send()
        return carry

    lax.fori_loop(0, taps, drain, 0)


def per_device(clips, out_grad, spatial_weight, temporal_weight):
    T, ND = lax.axis_size("tensor"), lax.axis_size("dp")
    _, frames, height, breadth, CL = clips.shape
    HW = height * breadth
    POS = frames * HW
    block = spatial_weight.shape[2] // ND
    stages = ND.bit_length() - 1
    taps = 12
    scale = 1.0 / float(POS * ND) ** 0.5
    hbm = pl.BlockSpec(memory_space=pl.ANY)
    vmem = pl.BlockSpec(memory_space=pltpu.VMEM)
    dma = pltpu.SemaphoreType.DMA
    wide = HW + 2 * breadth
    scratch = [
        pltpu.VMEM((9, T, CL, CL), BF16),
        pltpu.VMEM((3, T, CL, CL), BF16),
        pltpu.VMEM((T, frames, wide, CL), BF16),
        pltpu.VMEM((T, frames, wide, CL), BF16),
        pltpu.VMEM((frames, wide, CL), BF16),
        pltpu.VMEM((POS + 2 * HW, CL), BF16),
        pltpu.VMEM((T, POS + 2 * HW, CL), BF16),
        pltpu.VMEM((POS, CL), F32),
        pltpu.VMEM((POS, CL), F32),
        pltpu.VMEM((POS, CL), F32),
        pltpu.VMEM((T - 1, POS, CL), BF16),
        pltpu.VMEM((T - 1, POS, CL), BF16),
        pltpu.VMEM((T - 1, POS, CL), BF16),
        pltpu.VMEM((CL, CL), BF16),
        pltpu.VMEM((SLOTS, ND, block, CL), BF16),
    ]
    scratch += [pltpu.VMEM((taps, ND >> (s + 1), block, CL), BF16) for s in range(stages)]
    scratch += [dma((3, T)), dma((2, T)), dma((2, T)), dma((2, T)), dma((2, T))]
    scratch += [dma((stages, taps)), dma((stages, taps))]
    mixed, clip_grad, grads = pl.pallas_call(
        functools.partial(kernel, T, ND, frames, height, breadth, scale),
        out_shape=(
            jax.ShapeDtypeStruct((POS, CL), BF16),
            jax.ShapeDtypeStruct((POS, CL), BF16),
            jax.ShapeDtypeStruct((taps, block, CL), BF16),
        ),
        in_specs=[vmem, hbm, hbm, hbm],
        out_specs=(vmem, vmem, vmem),
        scratch_shapes=scratch,
        compiler_params=pltpu.CompilerParams(
            collective_id=0, has_side_effects=True, vmem_limit_bytes=63 * 1024 * 1024
        ),
        cost_estimate=pl.CostEstimate(
            flops=24 * POS * 3 * T * CL * CL, bytes_accessed=20 * 2**20, transcendentals=4 * POS * CL
        ),
    )(
        clips.reshape(POS, CL),
        out_grad.reshape(POS, CL),
        spatial_weight.reshape(9, T * CL, CL),
        temporal_weight,
    )
    spatial = jnp.transpose(grads[3:].reshape(3, 3, block, CL), (1, 0, 2, 3))
    return (
        mixed.reshape(clips.shape),
        clip_grad.reshape(clips.shape),
        spatial,
        jnp.transpose(grads[:3], (0, 2, 1)),
    )


def solution(mesh):
    placed = (
        P("dp", None, None, None, "tensor"),
        P("dp", None, None, None, "tensor"),
        P(None, None, None, "tensor"),
        P(None, "tensor", None),
    )
    return jax.shard_map(
        per_device,
        mesh=mesh,
        in_specs=placed,
        out_specs=(
            P("dp", None, None, None, "tensor"),
            P("dp", None, None, None, "tensor"),
            P(None, None, "dp", "tensor"),
            P(None, "tensor", "dp"),
        ),
        check_vma=False,
    )
```

```python
import functools

import jax
import jax.numpy as jnp
from jax import lax
from jax.experimental import pallas as pl
from jax.experimental.pallas import tpu as pltpu
from jax.sharding import PartitionSpec as P

GS = 32
SLOTS = 3
MESH = pl.DeviceIdType.MESH
F32, BF16 = jnp.float32, jnp.bfloat16
NN = (((1,), (0,)), ((), ()))
NT = (((1,), (1,)), ((), ()))
TN = (((0,), (0,)), ((), ()))


def dot(left, right, dims):
    return lax.dot_general(left, right, dims, preferred_element_type=F32)


def bits_reversed(value, size):
    result, step = 0, 1
    while step < size:
        result = result * 2 + (value // step) % 2
        step *= 2
    return result


def kernel(
    T, ND, frames, height, breadth, scale,
    clips, og_in, sw_in, tw_in,
    mixed, cgrad, wgrad, tgrad,
    sw, tw, first, shifted, gradsp, second, og, acc, gsec, own, ysend, fsend, tgot, fgot, same, gbuf, *rest,
):
    stages = ND.bit_length() - 1
    got = rest[:stages]
    load_sem, hf_sem, og_sem, to_sem, gf_sem, rs_send, rs_recv = rest[stages:]
    HW = height * breadth
    POS = frames * HW
    CL = clips.shape[1]
    block = wgrad.shape[1]
    early, half = frames // 4, frames // 2
    per_slot = CL // block
    me_t = lax.axis_index("tensor")
    me_d = lax.axis_index("dp")
    peers = [lax.rem(me_t + j, T) for j in range(T)]
    owners = [lax.rem(me_t - j + T, T) for j in range(T)]
    bit = [lax.rem(me_d // (1 << s), 2) for s in range(stages)]
    partner = [me_d + (1 - 2 * bit[s]) * (1 << s) for s in range(stages)]

    loads = []
    for j in range(T):
        rows = pl.ds(pl.multiple_of(owners[j] * CL, CL), CL)
        loads.append(pltpu.make_async_copy(sw_in.at[:, rows, :], sw.at[:, j], load_sem.at[0, j]))
        loads.append(pltpu.make_async_copy(tw_in.at[:, :, rows], tw.at[:, j], load_sem.at[1, j]))
    og_load = pltpu.make_async_copy(og_in, og.at[0, pl.ds(HW, POS)], load_sem.at[2, 0])
    og_load.start()
    for load in loads:
        load.start()

    barrier = pltpu.get_barrier_semaphore()
    for j in range(1, T):
        pl.semaphore_signal(barrier, inc=1, device_id={"tensor": peers[j]}, device_id_type=MESH)
    for s in range(stages):
        pl.semaphore_signal(barrier, inc=1, device_id={"dp": partner[s]}, device_id_type=MESH)

    edge = jnp.zeros((frames, breadth, CL), BF16)
    frame = jnp.zeros((HW, CL), BF16)
    for j in range(T):
        first[j, :, :breadth, :] = edge
        first[j, :, breadth + HW :, :] = edge
        og[j, :HW, :] = frame
        og[j, HW + POS :, :] = frame
    gradsp[:, :breadth, :] = edge
    gradsp[:, breadth + HW :, :] = edge
    second[:HW, :] = frame
    second[HW + POS :, :] = frame
    same[...] = jnp.where(
        lax.broadcasted_iota(jnp.int32, (CL, CL), 0) // GS
        == lax.broadcasted_iota(jnp.int32, (CL, CL), 1) // GS,
        1.0,
        0.0,
    ).astype(BF16)

    def group_mean(total):
        high = total.astype(BF16).astype(F32)
        middle = (total - high).astype(BF16).astype(F32)
        low = total - high - middle
        row = lax.broadcasted_iota(jnp.int32, (16, CL), 0)
        terms = jnp.where(row == 0, high, jnp.where(row == 1, middle, jnp.where(row == 2, low, 0.0)))
        summed = dot(terms.astype(BF16), same[...], NN)
        return jnp.sum(summed, axis=0, keepdims=True) * (1.0 / (GS * POS))

    def over_frames(body, count):
        zero = tuple(jnp.zeros((1, CL), F32) for _ in range(count))

        def step(f, sums):
            return tuple(a + jnp.sum(v, axis=0, keepdims=True) for a, v in zip(sums, body(f)))

        return lax.fori_loop(0, frames, step, zero)

    def rows_of(f, offset=0):
        return pl.ds(pl.multiple_of(f * HW + offset, HW), HW)

    def statistics(load):
        center = group_mean(over_frames(lambda f: (load(f),), 1)[0])

        def squares(f):
            offsets = load(f) - center
            return (offsets * offsets,)

        spread = group_mean(over_frames(squares, 1)[0])
        return center, lax.rsqrt(spread + 1e-05)

    def sigmoid(u):
        return 1.0 / (1.0 + jnp.exp(-u))

    def slope(u):
        s = sigmoid(u)
        return s * (1.0 + u * (1.0 - s))

    def pull_back(load, center, rate, grad, put):
        def sums(f):
            unit = (load(f) - center) * rate
            d = grad(f) * slope(unit)
            return d, d * unit

        a, b = over_frames(sums, 2)
        a, b = group_mean(a), group_mean(b)

        def write(f, carry):
            unit = (load(f) - center) * rate
            d = grad(f) * slope(unit)
            put(f, rate * (d - a - unit * b))
            return carry

        lax.fori_loop(0, frames, write, 0)

    def remote(source, target, sends, receives, device):
        return pltpu.make_async_remote_copy(
            src_ref=source, dst_ref=target, send_sem=sends, recv_sem=receives,
            device_id=device, device_id_type=MESH,
        )

    middle = pl.ds(HW, POS)
    og_copies = []
    for j, part in [(j, part) for part in range(2) for j in range(1, T)]:
        some = pl.ds(HW * (1 + early * part), HW * (frames - early if part else early))
        og_copies.append(
            remote(og.at[0, some], og.at[j, some], og_sem.at[part, j], og_sem.at[2 + part, j], {"tensor": peers[j]})
        )
    og_load.wait()
    pl.semaphore_wait(barrier, T - 1 + stages)
    for copy in og_copies[: T - 1]:
        copy.start()

    load_clip = lambda f: clips[rows_of(f), :].astype(F32)
    center1, rate1 = statistics(load_clip)
    inside = pl.ds(breadth, HW)

    def put_first(f, carry):
        unit = (load_clip(f) - center1) * rate1
        first[0, f, inside, :] = (unit * sigmoid(unit)).astype(BF16)
        return carry

    lax.fori_loop(0, frames, put_first, 0)
    hf_copies = []
    for j, part in [(j, part) for part in range(2) for j in range(1, T)]:
        some = pl.ds(part * half, frames - half if part else half)
        hf_copies.append(
            remote(first.at[0, some, inside, :], first.at[j, some, inside, :],
                   hf_sem.at[part, j], hf_sem.at[2 + part, j], {"tensor": peers[j]})
        )
        hf_copies[-1].start()
    for copy in og_copies[T - 1 :]:
        copy.start()
    for load in loads:
        load.wait()

    def shift(load, target, column, begin=0, end=frames):
        wide = HW + 2 * breadth
        at = lax.rem(lax.broadcasted_iota(jnp.int32, (wide, CL), 0), breadth)
        keep = at != (0 if column == 0 else breadth - 1)

        def step(f, carry):
            moved = pltpu.roll(load(f).astype(F32), 1 if column == 0 else wide - 1, 0)
            shifted[target, f] = jnp.where(keep, moved, 0.0).astype(BF16)
            return carry

        lax.fori_loop(begin, end, step, 0)

    def window(ref, slot, a, begin=0, end=frames):
        rows = pl.ds(pl.multiple_of(a * breadth, breadth), HW)
        if slot is None:
            return ref[begin:end, rows, :].reshape((end - begin) * HW, CL)
        return ref[slot, begin:end, rows, :].reshape((end - begin) * HW, CL)

    def conv_slot(j, begin=0, end=frames):
        out = pl.ds(begin * HW, (end - begin) * HW)
        for column in range(3):
            if column == 1:
                ref = first
            else:
                ref = shifted
                shift(lambda f: first[j, f], j, column, begin, end)

            def tap(a, carry, ref=ref, column=column):
                acc[out, :] += dot(window(ref, j, a, begin, end), sw[a * 3 + column, j], NN)
                return carry

            lax.fori_loop(0, 3, tap, 0)

    acc[...] = jnp.zeros_like(acc)
    conv_slot(0)
    for part in range(2):
        for j in range(1, T):
            hf_copies[part * (T - 1) + j - 1].wait_recv()
            conv_slot(j, part * half, frames if part else half)

    load_out = lambda f: acc[rows_of(f), :]
    center2, rate2 = statistics(load_out)

    def put_second(f, carry):
        unit = (load_out(f) - center2) * rate2
        second[rows_of(f, HW), :] = (unit * sigmoid(unit)).astype(BF16)
        return carry

    lax.fori_loop(0, frames, put_second, 0)

    def temporal(j, target):
        def tap(k, carry):
            target[...] += dot(second[pl.ds(pl.multiple_of(k * HW, HW), POS), :], tw[k, j], NN)
            return carry

        target[...] = jnp.zeros_like(target)
        lax.fori_loop(0, 3, tap, 0)

    to_copies, gf_copies = [], []
    for j in range(1, T):
        temporal(j, own)
        ysend[j - 1] = own[...].astype(BF16)
        to_copies.append(
            remote(ysend.at[j - 1], tgot.at[j - 1], to_sem.at[0, j], to_sem.at[1, j], {"tensor": owners[j]})
        )
        to_copies[-1].start()

    def back_slot(j):
        def tap(k, carry):
            rows = pl.ds(pl.multiple_of((2 - k) * HW, HW), POS)
            gsec[...] += dot(og[j, rows, :], tw[k, j], NT)
            return carry

        lax.fori_loop(0, 3, tap, 0)

    taps = wgrad.shape[0] + tgrad.shape[0]
    columns = (1, 0, 2)

    def source(s, n, half):
        size = ND >> (s + 1)
        rows = pl.ds(half * size, size)
        return gbuf.at[lax.rem(n, SLOTS), rows] if s == 0 else got[s - 1].at[n, rows]

    def exchange(s, n):
        return remote(source(s, n, 1 - bit[s]), got[s].at[n], rs_send.at[s, n], rs_recv.at[s, n],
                      {"dp": partner[s]})

    def advance(s, n):
        exchange(s - 1, n).wait_recv()
        total = got[s - 1][n].astype(F32) + source(s - 1, n, bit[s - 1])[...].astype(F32)
        if s < stages:
            got[s - 1][n] = total.astype(BF16)
            exchange(s, n).start()
        else:
            value = (total * scale).reshape(block, CL).astype(BF16)
            if n < 3:
                tgrad[n] = value
            else:
                wgrad[(n - 3) % 3 * 3 + columns[(n - 3) // 3]] = value

    def emit(n, slots):
        @pl.when(n >= SLOTS)
        def _():
            exchange(0, n - SLOTS).wait_send()

        for j in range(T):
            place = bits_reversed(owners[j], T)
            product = slots(j)
            for b in range(per_slot):
                gbuf[lax.rem(n, SLOTS), bits_reversed(b, per_slot) * T + place] = (
                    product[b * block : (b + 1) * block].astype(BF16)
                )
        exchange(0, n).start()

        @pl.when(n >= 1)
        def _():
            advance(1, n - 1)

    for copy in og_copies:
        copy.wait_recv()

    def temporal_tap(k, carry):
        rows = pl.ds(pl.multiple_of(k * HW, HW), POS)
        emit(k, lambda j: dot(og[j, middle, :], second[rows, :], TN))
        return carry

    lax.fori_loop(0, 3, temporal_tap, 0)

    gsec[...] = jnp.zeros_like(gsec)
    for j in range(T):
        back_slot(j)

    def put_gradsp(f, value):
        gradsp[f, inside, :] = value.astype(BF16)

    pull_back(load_out, center2, rate2, lambda f: gsec[rows_of(f), :], put_gradsp)

    done = {s: 0 for s in range(2, stages + 1)}

    def move(s, upto):
        for n in range(done[s], min(upto, taps)):
            advance(s, n)
        done[s] = max(done[s], min(upto, taps))

    def pace(upto):
        for s in range(2, stages + 1):
            move(s, upto - (s - 2))

    def spatial_taps(place):
        column = columns[place]
        if column == 1:
            ref = first
        else:
            ref = shifted
            for j in range(T):
                shift(lambda f, j=j: first[j, f], j, column)

        def tap(a, carry):
            emit(3 + place * 3 + a, lambda j: dot(window(ref, j, a), window(gradsp, None, 1), TN))
            return carry

        lax.fori_loop(0, 3, tap, 0)

    def grad_slot(j):
        acc[...] = jnp.zeros_like(acc)
        for column in range(3):
            if column == 1:
                ref, slot = gradsp, None
            else:
                ref, slot = shifted, 0
                shift(lambda f: gradsp[f], 0, column)

            def tap(a, carry, ref=ref, slot=slot, column=column):
                acc[...] += dot(window(ref, slot, a), sw[(2 - a) * 3 + 2 - column, j], NT)
                return carry

            lax.fori_loop(0, 3, tap, 0)

    spatial_taps(0)
    pace(3)
    for j in range(1, T):
        grad_slot(j)
        fsend[j - 1] = acc[...].astype(BF16)
        gf_copies.append(
            remote(fsend.at[j - 1], fgot.at[j - 1], gf_sem.at[0, j], gf_sem.at[1, j], {"tensor": owners[j]})
        )
        gf_copies[-1].start()
    pace(4)
    spatial_taps(1)
    pace(6)
    spatial_taps(2)
    advance(1, taps - 1)
    pace(7)
    grad_slot(0)
    pace(9)
    temporal(0, own)

    for j in range(1, T):
        to_copies[j - 1].wait_recv()

    def put_mixed(f, carry):
        rows = rows_of(f)
        total = load_clip(f) + own[rows, :]
        for j in range(1, T):
            total = total + tgot[j - 1, rows, :].astype(F32)
        mixed[rows, :] = total.astype(BF16)
        return carry

    lax.fori_loop(0, frames, put_mixed, 0)
    pace(10)

    for j in range(1, T):
        gf_copies[j - 1].wait_recv()

    def grad_first(f):
        total = acc[rows_of(f), :]
        for j in range(1, T):
            total = total + fgot[j - 1, rows_of(f), :].astype(F32)
        return total

    def put_clip(f, value):
        cgrad[rows_of(f), :] = (og[0, rows_of(f, HW), :].astype(F32) + value).astype(BF16)

    pull_back(load_clip, center1, rate1, grad_first, put_clip)

    for n in range(10, taps + stages):
        pace(n + 1)

    for copy in hf_copies + og_copies + to_copies + gf_copies:
        copy.wait_send()
    for n in range(max(0, taps - SLOTS), taps):
        exchange(0, n).wait_send()

    def drain(n, carry):
        for s in range(1, stages):
            exchange(s, n).wait_send()
        return carry

    lax.fori_loop(0, taps, drain, 0)


def per_device(clips, out_grad, spatial_weight, temporal_weight):
    T, ND = lax.axis_size("tensor"), lax.axis_size("dp")
    _, frames, height, breadth, CL = clips.shape
    HW = height * breadth
    POS = frames * HW
    block = spatial_weight.shape[2] // ND
    stages = ND.bit_length() - 1
    taps = 12
    scale = 1.0 / float(POS * ND) ** 0.5
    hbm = pl.BlockSpec(memory_space=pl.ANY)
    vmem = pl.BlockSpec(memory_space=pltpu.VMEM)
    dma = pltpu.SemaphoreType.DMA
    wide = HW + 2 * breadth
    scratch = [
        pltpu.VMEM((9, T, CL, CL), BF16),
        pltpu.VMEM((3, T, CL, CL), BF16),
        pltpu.VMEM((T, frames, wide, CL), BF16),
        pltpu.VMEM((T, frames, wide, CL), BF16),
        pltpu.VMEM((frames, wide, CL), BF16),
        pltpu.VMEM((POS + 2 * HW, CL), BF16),
        pltpu.VMEM((T, POS + 2 * HW, CL), BF16),
        pltpu.VMEM((POS, CL), F32),
        pltpu.VMEM((POS, CL), F32),
        pltpu.VMEM((POS, CL), F32),
        pltpu.VMEM((T - 1, POS, CL), BF16),
        pltpu.VMEM((T - 1, POS, CL), BF16),
        pltpu.VMEM((T - 1, POS, CL), BF16),
        pltpu.VMEM((T - 1, POS, CL), BF16),
        pltpu.VMEM((CL, CL), BF16),
        pltpu.VMEM((SLOTS, ND, block, CL), BF16),
    ]
    scratch += [pltpu.VMEM((taps, ND >> (s + 1), block, CL), BF16) for s in range(stages)]
    scratch += [dma((3, T)), dma((4, T)), dma((4, T)), dma((2, T)), dma((2, T))]
    scratch += [dma((stages, taps)), dma((stages, taps))]
    mixed, clip_grad, spatial, temporal = pl.pallas_call(
        functools.partial(kernel, T, ND, frames, height, breadth, scale),
        out_shape=(
            jax.ShapeDtypeStruct((POS, CL), BF16),
            jax.ShapeDtypeStruct((POS, CL), BF16),
            jax.ShapeDtypeStruct((taps - 3, block, CL), BF16),
            jax.ShapeDtypeStruct((3, block, CL), BF16),
        ),
        in_specs=[vmem, hbm, hbm, hbm],
        out_specs=(vmem, vmem, vmem, vmem),
        scratch_shapes=scratch,
        compiler_params=pltpu.CompilerParams(
            collective_id=0, has_side_effects=True, vmem_limit_bytes=63 * 1024 * 1024
        ),
        cost_estimate=pl.CostEstimate(
            flops=24 * POS * 3 * T * CL * CL, bytes_accessed=20 * 2**20, transcendentals=4 * POS * CL
        ),
    )(
        clips.reshape(POS, CL),
        out_grad.reshape(POS, CL),
        spatial_weight.reshape(9, T * CL, CL),
        temporal_weight,
    )
    return (
        mixed.reshape(clips.shape),
        clip_grad.reshape(clips.shape),
        spatial.reshape(3, 3, block, CL),
        jnp.transpose(temporal, (0, 2, 1)),
    )


def solution(mesh):
    placed = (
        P("dp", None, None, None, "tensor"),
        P("dp", None, None, None, "tensor"),
        P(None, None, None, "tensor"),
        P(None, "tensor", None),
    )
    return jax.shard_map(
        per_device,
        mesh=mesh,
        in_specs=placed,
        out_specs=(
            P("dp", None, None, None, "tensor"),
            P("dp", None, None, None, "tensor"),
            P(None, None, "dp", "tensor"),
            P(None, "tensor", "dp"),
        ),
        check_vma=False,
    )
```

```python
import functools

import jax
import jax.numpy as jnp
from jax import lax
from jax.experimental import pallas as pl
from jax.experimental.pallas import tpu as pltpu
from jax.sharding import PartitionSpec as P

GS = 32
SLOTS = 3
MESH = pl.DeviceIdType.MESH
F32, BF16 = jnp.float32, jnp.bfloat16
NN = (((1,), (0,)), ((), ()))
NT = (((1,), (1,)), ((), ()))


def dot(left, right, dims):
    return lax.dot_general(left, right, dims, preferred_element_type=F32)


def bits_reversed(value, size):
    result, step = 0, 1
    while step < size:
        result = result * 2 + (value // step) % 2
        step *= 2
    return result


def kernel(
    T, ND, frames, height, breadth, scale,
    clips, og_in, sw_in, tw_in,
    mixed, cgrad, wgrad, tgrad,
    sw, tw, first, shifted, gradsp, second, og, first_t, og_t, acc, gsec, own, ysend, fsend, tgot, fgot, same, gbuf, *rest,
):
    stages = ND.bit_length() - 1
    got = rest[:stages]
    load_sem, hf_sem, og_sem, to_sem, gf_sem, rs_send, rs_recv = rest[stages:]
    HW = height * breadth
    POS = frames * HW
    CL = clips.shape[1]
    block = wgrad.shape[1]
    half = frames // 2
    per_slot = CL // block
    me_t = lax.axis_index("tensor")
    me_d = lax.axis_index("dp")
    peers = [lax.rem(me_t + j, T) for j in range(T)]
    owners = [lax.rem(me_t - j + T, T) for j in range(T)]
    bit = [lax.rem(me_d // (1 << s), 2) for s in range(stages)]
    partner = [me_d + (1 - 2 * bit[s]) * (1 << s) for s in range(stages)]

    loads = []
    for j in range(T):
        rows = pl.ds(pl.multiple_of(owners[j] * CL, CL), CL)
        loads.append(pltpu.make_async_copy(sw_in.at[:, rows, :], sw.at[:, j], load_sem.at[0, j]))
        loads.append(pltpu.make_async_copy(tw_in.at[:, :, rows], tw.at[:, j], load_sem.at[1, j]))
    og_load = pltpu.make_async_copy(og_in, og.at[0, pl.ds(HW, POS)], load_sem.at[2, 0])
    og_load.start()
    for load in loads:
        load.start()

    barrier = pltpu.get_barrier_semaphore()
    for j in range(1, T):
        pl.semaphore_signal(barrier, inc=1, device_id={"tensor": peers[j]}, device_id_type=MESH)
    for s in range(stages):
        pl.semaphore_signal(barrier, inc=1, device_id={"dp": partner[s]}, device_id_type=MESH)

    edge = jnp.zeros((frames, breadth, CL), BF16)
    frame = jnp.zeros((HW, CL), BF16)
    for j in range(T):
        first[j, :, :breadth, :] = edge
        first[j, :, breadth + HW :, :] = edge
        og[j, :HW, :] = frame
        og[j, HW + POS :, :] = frame
    gradsp[:, :breadth, :] = edge
    gradsp[:, breadth + HW :, :] = edge
    second[:HW, :] = frame
    second[HW + POS :, :] = frame
    same[...] = jnp.where(
        lax.broadcasted_iota(jnp.int32, (CL, CL), 0) // GS
        == lax.broadcasted_iota(jnp.int32, (CL, CL), 1) // GS,
        1.0,
        0.0,
    ).astype(BF16)

    def group_mean(total):
        high = total.astype(BF16).astype(F32)
        middle = (total - high).astype(BF16).astype(F32)
        low = total - high - middle
        row = lax.broadcasted_iota(jnp.int32, (16, CL), 0)
        terms = jnp.where(row == 0, high, jnp.where(row == 1, middle, jnp.where(row == 2, low, 0.0)))
        summed = dot(terms.astype(BF16), same[...], NN)
        return jnp.sum(summed, axis=0, keepdims=True) * (1.0 / (GS * POS))

    def over_frames(body, count):
        zero = tuple(jnp.zeros((1, CL), F32) for _ in range(count))

        def step(f, sums):
            return tuple(a + jnp.sum(v, axis=0, keepdims=True) for a, v in zip(sums, body(f)))

        return lax.fori_loop(0, frames, step, zero)

    def rows_of(f, offset=0):
        return pl.ds(pl.multiple_of(f * HW + offset, HW), HW)

    def statistics(load):
        center = group_mean(over_frames(lambda f: (load(f),), 1)[0])

        def squares(f):
            offsets = load(f) - center
            return (offsets * offsets,)

        spread = group_mean(over_frames(squares, 1)[0])
        return center, lax.rsqrt(spread + 1e-05)

    def sigmoid(u):
        return 1.0 / (1.0 + jnp.exp(-u))

    def slope(u):
        s = sigmoid(u)
        return s * (1.0 + u * (1.0 - s))

    def pull_back(load, center, rate, grad, put):
        def sums(f):
            unit = (load(f) - center) * rate
            d = grad(f) * slope(unit)
            return d, d * unit

        a, b = over_frames(sums, 2)
        a, b = group_mean(a), group_mean(b)

        def write(f, carry):
            unit = (load(f) - center) * rate
            d = grad(f) * slope(unit)
            put(f, rate * (d - a - unit * b))
            return carry

        lax.fori_loop(0, frames, write, 0)

    def remote(source, target, sends, receives, device):
        return pltpu.make_async_remote_copy(
            src_ref=source, dst_ref=target, send_sem=sends, recv_sem=receives,
            device_id=device, device_id_type=MESH,
        )

    middle = pl.ds(HW, POS)
    og_copies = []
    for j in range(1, T):
        og_copies.append(
            remote(og.at[0, middle], og.at[j, middle], og_sem.at[0, j], og_sem.at[1, j], {"tensor": peers[j]})
        )
    og_load.wait()

    load_clip = lambda f: clips[rows_of(f), :].astype(F32)
    center1, rate1 = statistics(load_clip)
    inside = pl.ds(breadth, HW)

    def put_first(f, carry):
        unit = (load_clip(f) - center1) * rate1
        first[0, f, inside, :] = (unit * sigmoid(unit)).astype(BF16)
        return carry

    lax.fori_loop(0, frames, put_first, 0)
    pl.semaphore_wait(barrier, T - 1 + stages)
    hf_copies = []
    for j, part in [(j, part) for part in range(2) for j in range(1, T)]:
        some = pl.ds(part * half, frames - half if part else half)
        hf_copies.append(
            remote(first.at[0, some, inside, :], first.at[j, some, inside, :],
                   hf_sem.at[part, j], hf_sem.at[2 + part, j], {"tensor": peers[j]})
        )
        hf_copies[-1].start()
    for copy in og_copies:
        copy.start()
    for load in loads:
        load.wait()

    def shift(load, target, column, begin=0, end=frames):
        wide = HW + 2 * breadth
        at = lax.rem(lax.broadcasted_iota(jnp.int32, (wide, CL), 0), breadth)
        keep = at != (0 if column == 0 else breadth - 1)

        def step(f, carry):
            moved = pltpu.roll(load(f).astype(F32), 1 if column == 0 else wide - 1, 0)
            shifted[target, f] = jnp.where(keep, moved, 0.0).astype(BF16)
            return carry

        lax.fori_loop(begin, end, step, 0)

    def window(ref, slot, a, begin=0, end=frames):
        rows = pl.ds(pl.multiple_of(a * breadth, breadth), HW)
        if slot is None:
            return ref[begin:end, rows, :].reshape((end - begin) * HW, CL)
        return ref[slot, begin:end, rows, :].reshape((end - begin) * HW, CL)

    def turn(load, target, j, begin=0, end=frames):
        def step(f, carry):
            target[j, :, rows_of(f)] = jnp.transpose(load(f))
            return carry

        lax.fori_loop(begin, end, step, 0)

    def turn_first(j, begin=0, end=frames):
        turn(lambda f: first[j, f, inside, :], first_t, j, begin, end)

    def turn_og(j):
        turn(lambda f: og[j, rows_of(f, HW), :], og_t, j)

    def conv_slot(j, begin=0, end=frames):
        out = pl.ds(begin * HW, (end - begin) * HW)
        for column in range(3):
            if column == 1:
                ref, slot = first, j
            else:
                ref, slot = shifted, 0
                shift(lambda f: first[j, f], 0, column, begin, end)

            def tap(a, carry, ref=ref, slot=slot, column=column):
                acc[out, :] += dot(window(ref, slot, a, begin, end), sw[a * 3 + column, j], NN)
                return carry

            lax.fori_loop(0, 3, tap, 0)

    acc[...] = jnp.zeros_like(acc)
    conv_slot(0)
    turn_first(0)
    turn_og(0)
    for part in range(2):
        for j in range(1, T):
            hf_copies[part * (T - 1) + j - 1].wait_recv()
            conv_slot(j, part * half, frames if part else half)

    load_out = lambda f: acc[rows_of(f), :]
    center2, rate2 = statistics(load_out)

    def put_second(f, carry):
        unit = (load_out(f) - center2) * rate2
        second[rows_of(f, HW), :] = (unit * sigmoid(unit)).astype(BF16)
        return carry

    lax.fori_loop(0, frames, put_second, 0)

    def temporal(j, target):
        def tap(k, carry):
            target[...] += dot(second[pl.ds(pl.multiple_of(k * HW, HW), POS), :], tw[k, j], NN)
            return carry

        target[...] = jnp.zeros_like(target)
        lax.fori_loop(0, 3, tap, 0)

    to_copies, gf_copies = [], []
    for j in range(1, T):
        temporal(j, own)
        ysend[j - 1] = own[...].astype(BF16)
        to_copies.append(
            remote(ysend.at[j - 1], tgot.at[j - 1], to_sem.at[0, j], to_sem.at[1, j], {"tensor": owners[j]})
        )
        to_copies[-1].start()

    for j in range(1, T):
        turn_first(j)

    def back_slot(j):
        def tap(k, carry):
            rows = pl.ds(pl.multiple_of((2 - k) * HW, HW), POS)
            gsec[...] += dot(og[j, rows, :], tw[k, j], NT)
            return carry

        lax.fori_loop(0, 3, tap, 0)

    taps = wgrad.shape[0] + tgrad.shape[0]
    columns = (1, 0, 2)

    def source(s, n, half):
        size = ND >> (s + 1)
        rows = pl.ds(half * size, size)
        return gbuf.at[lax.rem(n, SLOTS), rows] if s == 0 else got[s - 1].at[n, rows]

    def exchange(s, n):
        return remote(source(s, n, 1 - bit[s]), got[s].at[n], rs_send.at[s, n], rs_recv.at[s, n],
                      {"dp": partner[s]})

    def advance(s, n):
        exchange(s - 1, n).wait_recv()
        total = got[s - 1][n].astype(F32) + source(s - 1, n, bit[s - 1])[...].astype(F32)
        if s < stages:
            got[s - 1][n] = total.astype(BF16)
            exchange(s, n).start()
        else:
            value = (total * scale).reshape(block, CL).astype(BF16)
            if n < 3:
                tgrad[n] = value
            else:
                wgrad[(n - 3) % 3 * 3 + columns[(n - 3) // 3]] = value

    def emit(n, slots):
        @pl.when(n >= SLOTS)
        def _():
            exchange(0, n - SLOTS).wait_send()

        for j in range(T):
            place = bits_reversed(owners[j], T)
            product = slots(j)
            for b in range(per_slot):
                gbuf[lax.rem(n, SLOTS), bits_reversed(b, per_slot) * T + place] = (
                    product[b * block : (b + 1) * block].astype(BF16)
                )
        exchange(0, n).start()

        @pl.when(n >= 1)
        def _():
            advance(1, n - 1)

    gsec[...] = jnp.zeros_like(gsec)
    back_slot(0)
    for j in range(1, T):
        og_copies[j - 1].wait_recv()
        turn_og(j)

    def temporal_tap(k, carry):
        rows = pl.ds(pl.multiple_of(k * HW, HW), POS)
        emit(k, lambda j: dot(og_t[j], second[rows, :], NN))
        return carry

    lax.fori_loop(0, 3, temporal_tap, 0)

    for j in range(1, T):
        back_slot(j)

    def put_gradsp(f, value):
        gradsp[f, inside, :] = value.astype(BF16)

    pull_back(load_out, center2, rate2, lambda f: gsec[rows_of(f), :], put_gradsp)

    done = {s: 0 for s in range(2, stages + 1)}

    def move(s, upto):
        for n in range(done[s], min(upto, taps)):
            advance(s, n)
        done[s] = max(done[s], min(upto, taps))

    def pace(upto):
        for s in range(2, stages + 1):
            move(s, upto - (s - 2))

    def spatial_taps(place):
        if columns[place] == 1:
            ref, slot = gradsp, None
        else:
            ref, slot = shifted, 0
            shift(lambda f: gradsp[f], 0, 2 - columns[place])

        def tap(a, carry):
            emit(3 + place * 3 + a, lambda j: dot(first_t[j], window(ref, slot, 2 - a), NN))
            return carry

        lax.fori_loop(0, 3, tap, 0)

    def grad_slot(j):
        acc[...] = jnp.zeros_like(acc)
        for column in range(3):
            if column == 1:
                ref, slot = gradsp, None
            else:
                ref, slot = shifted, 0
                shift(lambda f: gradsp[f], 0, column)

            def tap(a, carry, ref=ref, slot=slot, column=column):
                acc[...] += dot(window(ref, slot, a), sw[(2 - a) * 3 + 2 - column, j], NT)
                return carry

            lax.fori_loop(0, 3, tap, 0)

    spatial_taps(0)
    pace(2)
    spatial_taps(1)
    pace(4)
    spatial_taps(2)
    advance(1, taps - 1)
    pace(5)
    for j in range(1, T):
        grad_slot(j)
        fsend[j - 1] = acc[...].astype(BF16)
        gf_copies.append(
            remote(fsend.at[j - 1], fgot.at[j - 1], gf_sem.at[0, j], gf_sem.at[1, j], {"tensor": owners[j]})
        )
        gf_copies[-1].start()
    pace(7)
    grad_slot(0)
    pace(8)
    temporal(0, own)

    for j in range(1, T):
        to_copies[j - 1].wait_recv()

    def put_mixed(f, carry):
        rows = rows_of(f)
        total = load_clip(f) + own[rows, :]
        for j in range(1, T):
            total = total + tgot[j - 1, rows, :].astype(F32)
        mixed[rows, :] = total.astype(BF16)
        return carry

    lax.fori_loop(0, frames, put_mixed, 0)
    pace(10)

    for j in range(1, T):
        gf_copies[j - 1].wait_recv()

    def grad_first(f):
        total = acc[rows_of(f), :]
        for j in range(1, T):
            total = total + fgot[j - 1, rows_of(f), :].astype(F32)
        return total

    def put_clip(f, value):
        cgrad[rows_of(f), :] = (og[0, rows_of(f, HW), :].astype(F32) + value).astype(BF16)

    pull_back(load_clip, center1, rate1, grad_first, put_clip)

    for n in range(10, taps + stages):
        pace(n + 1)

    for copy in hf_copies + og_copies + to_copies + gf_copies:
        copy.wait_send()
    for n in range(max(0, taps - SLOTS), taps):
        exchange(0, n).wait_send()

    def drain(n, carry):
        for s in range(1, stages):
            exchange(s, n).wait_send()
        return carry

    lax.fori_loop(0, taps, drain, 0)


def per_device(clips, out_grad, spatial_weight, temporal_weight):
    T, ND = lax.axis_size("tensor"), lax.axis_size("dp")
    _, frames, height, breadth, CL = clips.shape
    HW = height * breadth
    POS = frames * HW
    block = spatial_weight.shape[2] // ND
    stages = ND.bit_length() - 1
    taps = 12
    scale = 1.0 / float(POS * ND) ** 0.5
    hbm = pl.BlockSpec(memory_space=pl.ANY)
    vmem = pl.BlockSpec(memory_space=pltpu.VMEM)
    dma = pltpu.SemaphoreType.DMA
    wide = HW + 2 * breadth
    scratch = [
        pltpu.VMEM((9, T, CL, CL), BF16),
        pltpu.VMEM((3, T, CL, CL), BF16),
        pltpu.VMEM((T, frames, wide, CL), BF16),
        pltpu.VMEM((1, frames, wide, CL), BF16),
        pltpu.VMEM((frames, wide, CL), BF16),
        pltpu.VMEM((POS + 2 * HW, CL), BF16),
        pltpu.VMEM((T, POS + 2 * HW, CL), BF16),
        pltpu.VMEM((T, CL, POS), BF16),
        pltpu.VMEM((T, CL, POS), BF16),
        pltpu.VMEM((POS, CL), F32),
        pltpu.VMEM((POS, CL), F32),
        pltpu.VMEM((POS, CL), F32),
        pltpu.VMEM((T - 1, POS, CL), BF16),
        pltpu.VMEM((T - 1, POS, CL), BF16),
        pltpu.VMEM((T - 1, POS, CL), BF16),
        pltpu.VMEM((T - 1, POS, CL), BF16),
        pltpu.VMEM((CL, CL), BF16),
        pltpu.VMEM((SLOTS, ND, block, CL), BF16),
    ]
    scratch += [pltpu.VMEM((taps, ND >> (s + 1), block, CL), BF16) for s in range(stages)]
    scratch += [dma((3, T)), dma((4, T)), dma((2, T)), dma((2, T)), dma((2, T))]
    scratch += [dma((stages, taps)), dma((stages, taps))]
    mixed, clip_grad, spatial, temporal = pl.pallas_call(
        functools.partial(kernel, T, ND, frames, height, breadth, scale),
        out_shape=(
            jax.ShapeDtypeStruct((POS, CL), BF16),
            jax.ShapeDtypeStruct((POS, CL), BF16),
            jax.ShapeDtypeStruct((taps - 3, block, CL), BF16),
            jax.ShapeDtypeStruct((3, block, CL), BF16),
        ),
        in_specs=[vmem, hbm, hbm, hbm],
        out_specs=(vmem, vmem, vmem, vmem),
        scratch_shapes=scratch,
        compiler_params=pltpu.CompilerParams(
            collective_id=0, has_side_effects=True, vmem_limit_bytes=63 * 1024 * 1024
        ),
        cost_estimate=pl.CostEstimate(
            flops=24 * POS * 3 * T * CL * CL, bytes_accessed=20 * 2**20, transcendentals=4 * POS * CL
        ),
    )(
        clips.reshape(POS, CL),
        out_grad.reshape(POS, CL),
        spatial_weight.reshape(9, T * CL, CL),
        temporal_weight,
    )
    return (
        mixed.reshape(clips.shape),
        clip_grad.reshape(clips.shape),
        spatial.reshape(3, 3, block, CL),
        jnp.transpose(temporal, (0, 2, 1)),
    )


def solution(mesh):
    placed = (
        P("dp", None, None, None, "tensor"),
        P("dp", None, None, None, "tensor"),
        P(None, None, None, "tensor"),
        P(None, "tensor", None),
    )
    return jax.shard_map(
        per_device,
        mesh=mesh,
        in_specs=placed,
        out_specs=(
            P("dp", None, None, None, "tensor"),
            P("dp", None, None, None, "tensor"),
            P(None, None, "dp", "tensor"),
            P(None, "tensor", "dp"),
        ),
        check_vma=False,
    )
```

```python
import functools

import jax
import jax.numpy as jnp
from jax import lax
from jax.experimental import pallas as pl
from jax.experimental.pallas import tpu as pltpu
from jax.sharding import PartitionSpec as P

GS = 32
SLOTS = 3
MESH = pl.DeviceIdType.MESH
F32, BF16 = jnp.float32, jnp.bfloat16
NN = (((1,), (0,)), ((), ()))
NT = (((1,), (1,)), ((), ()))


def dot(left, right, dims):
    return lax.dot_general(left, right, dims, preferred_element_type=F32)


def kernel(
    T, ND, frames, height, breadth, scale,
    clips, og_in, sw_in, tw_in,
    mixed, cgrad, wgrad, tgrad,
    sw, tw, first, shifted, gradsp, second, og, first_t, og_t, acc, gsec, own, ysend, fsend, tgot, fgot, same, gbuf, *rest,
):
    stages = ND.bit_length() - 1
    got = rest[:stages]
    load_sem, hf_sem, og_sem, to_sem, gf_sem, rs_send, rs_recv = rest[stages:]
    HW = height * breadth
    POS = frames * HW
    CL = clips.shape[1]
    block = wgrad.shape[1]
    per_slot = CL // block
    me_t = lax.axis_index("tensor")
    me_d = lax.axis_index("dp")
    peers = [lax.rem(me_t + j, T) for j in range(T)]
    owners = [lax.rem(me_t - j + T, T) for j in range(T)]
    bit = [lax.rem(me_d // (1 << s), 2) for s in range(stages)]
    partner = [me_d + (1 - 2 * bit[s]) * (1 << s) for s in range(stages)]

    loads = []
    for j in range(T):
        rows = pl.ds(pl.multiple_of(owners[j] * CL, CL), CL)
        loads.append(pltpu.make_async_copy(sw_in.at[:, rows, :], sw.at[:, j], load_sem.at[0, j]))
        loads.append(pltpu.make_async_copy(tw_in.at[:, :, rows], tw.at[:, j], load_sem.at[1, j]))
    og_load = pltpu.make_async_copy(og_in, og.at[0, pl.ds(HW, POS)], load_sem.at[2, 0])
    og_load.start()
    for load in loads:
        load.start()

    barrier = pltpu.get_barrier_semaphore()
    for j in range(1, T):
        pl.semaphore_signal(barrier, inc=1, device_id={"tensor": peers[j]}, device_id_type=MESH)
    for s in range(stages):
        pl.semaphore_signal(barrier, inc=1, device_id={"dp": partner[s]}, device_id_type=MESH)

    edge = jnp.zeros((frames, breadth, CL), BF16)
    frame = jnp.zeros((HW, CL), BF16)
    for j in range(T):
        first[j, :, :breadth, :] = edge
        first[j, :, breadth + HW :, :] = edge
        og[j, :HW, :] = frame
        og[j, HW + POS :, :] = frame
    gradsp[:, :breadth, :] = edge
    gradsp[:, breadth + HW :, :] = edge
    second[:HW, :] = frame
    second[HW + POS :, :] = frame
    same[...] = jnp.where(
        lax.broadcasted_iota(jnp.int32, (CL, CL), 0) // GS
        == lax.broadcasted_iota(jnp.int32, (CL, CL), 1) // GS,
        1.0,
        0.0,
    ).astype(BF16)

    def group_mean(total):
        high = total.astype(BF16).astype(F32)
        middle = (total - high).astype(BF16).astype(F32)
        low = total - high - middle
        row = lax.broadcasted_iota(jnp.int32, (16, CL), 0)
        terms = jnp.where(row == 0, high, jnp.where(row == 1, middle, jnp.where(row == 2, low, 0.0)))
        summed = dot(terms.astype(BF16), same[...], NN)
        return jnp.sum(summed, axis=0, keepdims=True) * (1.0 / (GS * POS))

    def over_frames(body, count):
        zero = tuple(jnp.zeros((1, CL), F32) for _ in range(count))

        def step(f, sums):
            return tuple(a + jnp.sum(v, axis=0, keepdims=True) for a, v in zip(sums, body(f)))

        return lax.fori_loop(0, frames, step, zero)

    def rows_of(f, offset=0):
        return pl.ds(pl.multiple_of(f * HW + offset, HW), HW)

    def statistics(load):
        center = group_mean(over_frames(lambda f: (load(f),), 1)[0])

        def squares(f):
            offsets = load(f) - center
            return (offsets * offsets,)

        spread = group_mean(over_frames(squares, 1)[0])
        return center, lax.rsqrt(spread + 1e-05)

    def sigmoid(u):
        return 1.0 / (1.0 + jnp.exp(-u))

    def slope(u):
        s = sigmoid(u)
        return s * (1.0 + u * (1.0 - s))

    def pull_back(load, center, rate, grad, put):
        def sums(f):
            unit = (load(f) - center) * rate
            d = grad(f) * slope(unit)
            return d, d * unit

        a, b = over_frames(sums, 2)
        a, b = group_mean(a), group_mean(b)

        def write(f, carry):
            unit = (load(f) - center) * rate
            d = grad(f) * slope(unit)
            put(f, rate * (d - a - unit * b))
            return carry

        lax.fori_loop(0, frames, write, 0)

    def remote(source, target, sends, receives, device):
        return pltpu.make_async_remote_copy(
            src_ref=source, dst_ref=target, send_sem=sends, recv_sem=receives,
            device_id=device, device_id_type=MESH,
        )

    middle = pl.ds(HW, POS)
    og_copies = []
    for j in range(1, T):
        og_copies.append(
            remote(og.at[0, middle], og.at[j, middle], og_sem.at[0, j], og_sem.at[1, j], {"tensor": peers[j]})
        )
    og_load.wait()

    load_clip = lambda f: clips[rows_of(f), :].astype(F32)
    center1, rate1 = statistics(load_clip)
    inside = pl.ds(breadth, HW)

    def put_first(f, carry):
        unit = (load_clip(f) - center1) * rate1
        first[0, f, inside, :] = (unit * sigmoid(unit)).astype(BF16)
        return carry

    lax.fori_loop(0, frames, put_first, 0)
    pl.semaphore_wait(barrier, T - 1 + stages)
    hf_copies = []
    for j in range(1, T):
        hf_copies.append(
            remote(first.at[0, :, inside, :], first.at[j, :, inside, :],
                   hf_sem.at[0, j], hf_sem.at[1, j], {"tensor": peers[j]})
        )
        hf_copies[-1].start()
    for copy in og_copies:
        copy.start()
    for load in loads:
        load.wait()

    def shift(load, target, column, begin=0, end=frames):
        wide = HW + 2 * breadth
        at = lax.rem(lax.broadcasted_iota(jnp.int32, (wide, CL), 0), breadth)
        keep = at != (0 if column == 0 else breadth - 1)

        def step(f, carry):
            moved = pltpu.roll(load(f).astype(F32), 1 if column == 0 else wide - 1, 0)
            shifted[target, f] = jnp.where(keep, moved, 0.0).astype(BF16)
            return carry

        lax.fori_loop(begin, end, step, 0)

    def window(ref, slot, a, begin=0, end=frames):
        rows = pl.ds(pl.multiple_of(a * breadth, breadth), HW)
        if slot is None:
            return ref[begin:end, rows, :].reshape((end - begin) * HW, CL)
        return ref[slot, begin:end, rows, :].reshape((end - begin) * HW, CL)

    def turn(load, target, j, begin=0, end=frames):
        def step(f, carry):
            target[j, :, rows_of(f)] = jnp.transpose(load(f))
            return carry

        lax.fori_loop(begin, end, step, 0)

    def turn_first(j, begin=0, end=frames):
        turn(lambda f: first[j, f, inside, :], first_t, j, begin, end)

    def turn_og(j):
        turn(lambda f: og[j, rows_of(f, HW), :], og_t, j)

    def conv_slot(j, begin=0, end=frames):
        out = pl.ds(begin * HW, (end - begin) * HW)
        for column in range(3):
            if column == 1:
                ref, slot = first, j
            else:
                ref, slot = shifted, 0
                shift(lambda f: first[j, f], 0, column, begin, end)

            def tap(a, carry, ref=ref, slot=slot, column=column):
                acc[out, :] += dot(window(ref, slot, a, begin, end), sw[a * 3 + column, j], NN)
                return carry

            lax.fori_loop(0, 3, tap, 0)

    acc[...] = jnp.zeros_like(acc)
    conv_slot(0)
    turn_first(0)
    turn_og(0)
    for j in range(1, T):
        hf_copies[j - 1].wait_recv()
        conv_slot(j)

    load_out = lambda f: acc[rows_of(f), :]
    center2, rate2 = statistics(load_out)

    def put_second(f, carry):
        unit = (load_out(f) - center2) * rate2
        second[rows_of(f, HW), :] = (unit * sigmoid(unit)).astype(BF16)
        return carry

    lax.fori_loop(0, frames, put_second, 0)

    def temporal(j, target):
        def tap(k, carry):
            target[...] += dot(second[pl.ds(pl.multiple_of(k * HW, HW), POS), :], tw[k, j], NN)
            return carry

        target[...] = jnp.zeros_like(target)
        lax.fori_loop(0, 3, tap, 0)

    to_copies, gf_copies = [], []
    for j in range(1, T):
        temporal(j, own)
        ysend[j - 1] = own[...].astype(BF16)
        to_copies.append(
            remote(ysend.at[j - 1], tgot.at[j - 1], to_sem.at[0, j], to_sem.at[1, j], {"tensor": owners[j]})
        )
        to_copies[-1].start()

    def back_slot(j):
        def tap(k, carry):
            rows = pl.ds(pl.multiple_of((2 - k) * HW, HW), POS)
            gsec[...] += dot(og[j, rows, :], tw[k, j], NT)
            return carry

        lax.fori_loop(0, 3, tap, 0)

    taps = wgrad.shape[0] + tgrad.shape[0]
    columns = (1, 0, 2)

    def swapped(n):
        return (n % 2) * (1 - (n // 2) % 2) if stages >= 3 else 0

    def pick(values, s, n):
        if stages < 3 or s not in (1, 2):
            return values[s]
        return values[s] + swapped(n) * (values[3 - s] - values[s])

    def position(j, b, n):
        digits = []
        for k in range(stages):
            low = (1 << k) < per_slot
            digits.append((b >> k) % 2 if low else lax.rem(owners[j] // ((1 << k) // per_slot), 2))
        place = sum(digit * (ND >> (k + 1)) for k, digit in enumerate(digits))
        if stages >= 3:
            place = place + swapped(n) * ((digits[2] - digits[1]) * (ND >> 3))
        return place

    def source(s, n, half):
        size = ND >> (s + 1)
        rows = pl.ds(half * size, size)
        return gbuf.at[lax.rem(n, SLOTS), rows] if s == 0 else got[s - 1].at[n, rows]

    def exchange(s, n):
        return remote(source(s, n, 1 - pick(bit, s, n)), got[s].at[n], rs_send.at[s, n], rs_recv.at[s, n],
                      {"dp": pick(partner, s, n)})

    def advance(s, n):
        exchange(s - 1, n).wait_recv()
        total = got[s - 1][n].astype(F32) + source(s - 1, n, pick(bit, s - 1, n))[...].astype(F32)
        if s < stages:
            got[s - 1][n] = total.astype(BF16)
            exchange(s, n).start()
        else:
            value = (total * scale).reshape(block, CL).astype(BF16)
            if n < 3:
                tgrad[n] = value
            else:
                wgrad[(n - 3) % 3 * 3 + columns[(n - 3) // 3]] = value

    def emit(n, slots):
        @pl.when(n >= SLOTS)
        def _():
            exchange(0, n - SLOTS).wait_send()

        for j in range(T):
            product = slots(j)
            for b in range(per_slot):
                gbuf[lax.rem(n, SLOTS), position(j, b, n)] = (
                    product[b * block : (b + 1) * block].astype(BF16)
                )
        exchange(0, n).start()

        @pl.when(n >= 1)
        def _():
            advance(1, n - 1)

    gsec[...] = jnp.zeros_like(gsec)
    back_slot(0)
    for j in range(1, T):
        og_copies[j - 1].wait_recv()
        turn_og(j)

    def temporal_tap(k, carry):
        rows = pl.ds(pl.multiple_of(k * HW, HW), POS)
        emit(k, lambda j: dot(og_t[j], second[rows, :], NN))
        return carry

    lax.fori_loop(0, 3, temporal_tap, 0)
    for j in range(1, T):
        turn_first(j)

    for j in range(1, T):
        back_slot(j)

    def put_gradsp(f, value):
        gradsp[f, inside, :] = value.astype(BF16)

    pull_back(load_out, center2, rate2, lambda f: gsec[rows_of(f), :], put_gradsp)

    done = {s: 0 for s in range(2, stages + 1)}

    def move(s, upto):
        for n in range(done[s], min(upto, taps)):
            advance(s, n)
        done[s] = max(done[s], min(upto, taps))

    def pace(upto):
        for s in range(2, stages + 1):
            move(s, upto - (s - 2))

    def spatial_taps(place):
        if columns[place] == 1:
            ref, slot = gradsp, None
        else:
            ref, slot = shifted, 0
            shift(lambda f: gradsp[f], 0, 2 - columns[place])

        def tap(a, carry):
            emit(3 + place * 3 + a, lambda j: dot(first_t[j], window(ref, slot, 2 - a), NN))
            return carry

        lax.fori_loop(0, 3, tap, 0)

    def grad_slot(j):
        acc[...] = jnp.zeros_like(acc)
        for column in range(3):
            if column == 1:
                ref, slot = gradsp, None
            else:
                ref, slot = shifted, 0
                shift(lambda f: gradsp[f], 0, column)

            def tap(a, carry, ref=ref, slot=slot, column=column):
                acc[...] += dot(window(ref, slot, a), sw[(2 - a) * 3 + 2 - column, j], NT)
                return carry

            lax.fori_loop(0, 3, tap, 0)

    spatial_taps(0)
    pace(2)
    spatial_taps(1)
    pace(3)
    for j in range(1, T):
        grad_slot(j)
        fsend[j - 1] = acc[...].astype(BF16)
        gf_copies.append(
            remote(fsend.at[j - 1], fgot.at[j - 1], gf_sem.at[0, j], gf_sem.at[1, j], {"tensor": owners[j]})
        )
        gf_copies[-1].start()
    pace(5)
    spatial_taps(2)
    advance(1, taps - 1)
    pace(6)
    grad_slot(0)
    pace(8)
    temporal(0, own)

    for j in range(1, T):
        to_copies[j - 1].wait_recv()

    def put_mixed(f, carry):
        rows = rows_of(f)
        total = load_clip(f) + own[rows, :]
        for j in range(1, T):
            total = total + tgot[j - 1, rows, :].astype(F32)
        mixed[rows, :] = total.astype(BF16)
        return carry

    lax.fori_loop(0, frames, put_mixed, 0)
    pace(10)

    for j in range(1, T):
        gf_copies[j - 1].wait_recv()

    def grad_first(f):
        total = acc[rows_of(f), :]
        for j in range(1, T):
            total = total + fgot[j - 1, rows_of(f), :].astype(F32)
        return total

    def put_clip(f, value):
        cgrad[rows_of(f), :] = (og[0, rows_of(f, HW), :].astype(F32) + value).astype(BF16)

    pull_back(load_clip, center1, rate1, grad_first, put_clip)

    for n in range(10, taps + stages):
        pace(n + 1)

    for copy in hf_copies + og_copies + to_copies + gf_copies:
        copy.wait_send()
    for n in range(max(0, taps - SLOTS), taps):
        exchange(0, n).wait_send()

    def drain(n, carry):
        for s in range(1, stages):
            exchange(s, n).wait_send()
        return carry

    lax.fori_loop(0, taps, drain, 0)


def per_device(clips, out_grad, spatial_weight, temporal_weight):
    T, ND = lax.axis_size("tensor"), lax.axis_size("dp")
    _, frames, height, breadth, CL = clips.shape
    HW = height * breadth
    POS = frames * HW
    block = spatial_weight.shape[2] // ND
    stages = ND.bit_length() - 1
    taps = 12
    scale = 1.0 / float(POS * ND) ** 0.5
    hbm = pl.BlockSpec(memory_space=pl.ANY)
    vmem = pl.BlockSpec(memory_space=pltpu.VMEM)
    dma = pltpu.SemaphoreType.DMA
    wide = HW + 2 * breadth
    scratch = [
        pltpu.VMEM((9, T, CL, CL), BF16),
        pltpu.VMEM((3, T, CL, CL), BF16),
        pltpu.VMEM((T, frames, wide, CL), BF16),
        pltpu.VMEM((1, frames, wide, CL), BF16),
        pltpu.VMEM((frames, wide, CL), BF16),
        pltpu.VMEM((POS + 2 * HW, CL), BF16),
        pltpu.VMEM((T, POS + 2 * HW, CL), BF16),
        pltpu.VMEM((T, CL, POS), BF16),
        pltpu.VMEM((T, CL, POS), BF16),
        pltpu.VMEM((POS, CL), F32),
        pltpu.VMEM((POS, CL), F32),
        pltpu.VMEM((POS, CL), F32),
        pltpu.VMEM((T - 1, POS, CL), BF16),
        pltpu.VMEM((T - 1, POS, CL), BF16),
        pltpu.VMEM((T - 1, POS, CL), BF16),
        pltpu.VMEM((T - 1, POS, CL), BF16),
        pltpu.VMEM((CL, CL), BF16),
        pltpu.VMEM((SLOTS, ND, block, CL), BF16),
    ]
    scratch += [pltpu.VMEM((taps, ND >> (s + 1), block, CL), BF16) for s in range(stages)]
    scratch += [dma((3, T)), dma((2, T)), dma((2, T)), dma((2, T)), dma((2, T))]
    scratch += [dma((stages, taps)), dma((stages, taps))]
    mixed, clip_grad, spatial, temporal = pl.pallas_call(
        functools.partial(kernel, T, ND, frames, height, breadth, scale),
        out_shape=(
            jax.ShapeDtypeStruct((POS, CL), BF16),
            jax.ShapeDtypeStruct((POS, CL), BF16),
            jax.ShapeDtypeStruct((taps - 3, block, CL), BF16),
            jax.ShapeDtypeStruct((3, block, CL), BF16),
        ),
        in_specs=[vmem, hbm, hbm, hbm],
        out_specs=(vmem, vmem, vmem, vmem),
        scratch_shapes=scratch,
        compiler_params=pltpu.CompilerParams(
            collective_id=0, has_side_effects=True, vmem_limit_bytes=63 * 1024 * 1024
        ),
        cost_estimate=pl.CostEstimate(
            flops=24 * POS * 3 * T * CL * CL, bytes_accessed=20 * 2**20, transcendentals=4 * POS * CL
        ),
    )(
        clips.reshape(POS, CL),
        out_grad.reshape(POS, CL),
        spatial_weight.reshape(9, T * CL, CL),
        temporal_weight,
    )
    return (
        mixed.reshape(clips.shape),
        clip_grad.reshape(clips.shape),
        spatial.reshape(3, 3, block, CL),
        jnp.transpose(temporal, (0, 2, 1)),
    )


def solution(mesh):
    placed = (
        P("dp", None, None, None, "tensor"),
        P("dp", None, None, None, "tensor"),
        P(None, None, None, "tensor"),
        P(None, "tensor", None),
    )
    return jax.shard_map(
        per_device,
        mesh=mesh,
        in_specs=placed,
        out_specs=(
            P("dp", None, None, None, "tensor"),
            P("dp", None, None, None, "tensor"),
            P(None, None, "dp", "tensor"),
            P(None, "tensor", "dp"),
        ),
        check_vma=False,
    )
```
